128 devices in a mesh: sub: 128 (over x, z, y, core).
Axes of the slice: x: 4, y: 4, z: 4, core: 2. Of those that a mesh axis runs over, the one named last changes fastest.
Arguments:
- gap_loads: bfloat16 [256, 2048, 128], P('sub')
- flexibility: bfloat16 [256, 2048, 2048], P('sub'), as said below
- corner_coupling: bfloat16 [256, 16, 2048], P('sub'), may hold values from -0.5 to 0.5
- corner_ids: int32 [256, 16], P('sub'), may hold values from 0 to 1023
- coarse_inverse: float32 [1024, 1024], P('sub'), as said below
- adjacency: int32 [256, 4], P('sub'), may hold values from 0 to 255, as said below
Outputs:
- multipliers: float32 [256, 2048, 128], P('sub')
- residual: float32 [256, 2048, 128], P('sub')
The draws below stay inside these ranges and needn't reach their ends.
Inputs may be any that keep to these rules, and one draw needn't show every extreme that they name: Subdomain s = d * 2 + i lies on device d. Its partner across face f lies on device d XOR 2^f, and the pairing is mutual: adjacency[adjacency[s, f], f] = s. Each flexibility[s] is symmetric positive definite. coarse_inverse is symmetric positive definite.
All inputs are finite; a program needn't handle non-finite values.
Results may differ from the reference program's by a relative error of at most 0.019.
Values may be sent and summed in bfloat16 or wider, within the bound.
A program may use at most 128 MiB of HBM per device.

```python
import jax
import jax.numpy as jnp
from jax import lax

NI = 2048
FACES = 4
NC = 16
ITERS = 3
SUB_DEV = 2
LOADS = 128
SUBS = 256
NCG = 1024
NF = 512
N_SUB = 128


def spd_block(key, order, low_diag, high_diag):
    diag_key = jax.random.fold_in(key, 11)
    body_key = jax.random.fold_in(key, 12)
    diagonal = jnp.exp(jax.random.uniform(diag_key, (order,), jnp.float32, jnp.log(low_diag), jnp.log(high_diag)))
    noise = jax.random.normal(body_key, (order, order), jnp.float32)
    sym = (noise + noise.T) * (0.3 / jnp.sqrt(2.0 * order))
    scaled = jnp.sqrt(diagonal)[:, None] * jnp.sqrt(diagonal)[None, :]
    return scaled * (jnp.eye(order, dtype=jnp.float32) + sym)


def draw_flexibility(key, part):
    upper_diag = 10.0

    def single(index):
        return spd_block(jax.random.fold_in(key, index), NI, 1.0, upper_diag).astype(jnp.bfloat16)
    return lax.map(single, jnp.arange(SUBS, dtype=jnp.int32))


def draw_coarse_inverse(key, part):
    upper_diag = 2.0
    return spd_block(jax.random.fold_in(key, 5), NCG, 0.5, upper_diag)


def draw_gap_loads(key, part):
    rising = 1.0 + 2.0 * jnp.arange(SUBS, dtype=jnp.float32) / max(SUBS - 1, 1)
    values = jax.random.normal(jax.random.fold_in(key, 1), (SUBS, NI, LOADS), jnp.float32) * rising[:, None, None]
    return values.astype(jnp.bfloat16)


def draw_adjacency(key, part):
    devices = jnp.arange(N_SUB, dtype=jnp.int32)
    columns = []
    for face_round in range(FACES):
        partner_dev = jnp.bitwise_xor(devices, 1 << face_round)
        lower = jnp.minimum(devices, partner_dev)
        round_key = jax.random.fold_in(key, face_round + 100)
        perms = jax.vmap(lambda low: jax.random.permutation(jax.random.fold_in(round_key, low), SUB_DEV))(lower).astype(jnp.int32)
        inverse = jnp.argsort(perms, axis=1, stable=True).astype(jnp.int32)
        slots = jnp.where((devices < partner_dev)[:, None], perms, inverse)
        columns.append((partner_dev[:, None] * SUB_DEV + slots).reshape(-1))
    return jnp.stack(columns, axis=1).astype(jnp.int32)


def set_ends(entries, key, least, top_value):
    shape = entries.shape
    index_at = [jax.random.randint(jax.random.fold_in(key, axis), (), 0, shape[axis]) for axis in range(len(shape))]
    entries = entries.at[tuple(index_at)].set(least)
    longest = shape.index(max(shape))
    index_at[longest] = (index_at[longest] + 1) % shape[longest]
    return entries.at[tuple(index_at)].set(top_value)


def block_scale(own_key, extent, pieces, smallest, high):
    level, own = 1.0, jax.random.fold_in(own_key, 6)
    for axis_at, shards_of in pieces:
        draws = jnp.exp(jax.random.uniform(jax.random.fold_in(own, axis_at), (shards_of,), jnp.float32, smallest / len(pieces), high / len(pieces)))
        level = level * jnp.repeat(draws, extent[axis_at] // shards_of).reshape([-1 if axis == axis_at else 1 for axis in range(len(extent))])
    return level


def centred(key, shape, width, most, split=(), kind=jnp.bfloat16):
    values = jax.random.normal(key, shape, jnp.float32) * width
    if len(split) > 0:
        values = block_scale(key, shape, split, -0.22, 0.18) * values
    return jnp.clip(values, min=-most, max=most).astype(kind)


def setup_inputs(seed: int = 0) -> dict:
    key_of = jax.random.split(jax.random.key(seed), 7)
    gap_loads = draw_gap_loads(jax.random.fold_in(key_of[6], 71), 0)
    flexibility = draw_flexibility(jax.random.fold_in(key_of[6], 71), 0)
    corner_coupling = centred(key_of[2], (SUBS, NC, NI), (NI // NC) ** -0.5, 0.5, ((0, 128),))
    corner_ids = set_ends(jax.random.randint(key_of[3], (SUBS, NC), 0, NCG), jax.random.fold_in(key_of[3], 1), 0, NCG - 1).astype(jnp.int32)
    coarse_inverse = draw_coarse_inverse(jax.random.fold_in(key_of[6], 71), 0)
    adjacency = draw_adjacency(jax.random.fold_in(key_of[6], 71), 0)
    return dict(gap_loads=gap_loads, flexibility=flexibility, corner_coupling=corner_coupling, corner_ids=corner_ids, coarse_inverse=coarse_inverse, adjacency=adjacency)


def jump(field, adjacency):
    whole = field.reshape(field.shape[0], FACES, NF, field.shape[2])
    face_index = jnp.arange(FACES, dtype=jnp.int32)[None, :]
    partner = whole[adjacency, face_index]
    return (whole - partner).reshape(field.shape)


def apply_operator(direction, flexibility, corner_coupling, corner_ids, coarse_inverse, adjacency):
    rounded = direction.astype(jnp.bfloat16)
    local_part = lax.map(lambda pair: jnp.dot(pair[0], pair[1], preferred_element_type=jnp.float32), (flexibility, rounded))
    corner_terms = lax.map(lambda pair: jnp.dot(pair[0], pair[1], preferred_element_type=jnp.float32), (corner_coupling, rounded))
    coarse_rhs = jnp.zeros((NCG, LOADS), jnp.float32).at[corner_ids.reshape(-1)].add(corner_terms.reshape(-1, LOADS))
    coarse_sol = jnp.dot(coarse_inverse, coarse_rhs, precision=lax.Precision.HIGHEST)
    corner_values = coarse_sol[corner_ids]
    total = local_part + jnp.einsum("skn,skr->snr", corner_coupling.astype(jnp.float32), corner_values, precision=lax.Precision.HIGHEST)
    return jump(total, adjacency)


def reference(gap_loads, flexibility, corner_coupling, corner_ids, coarse_inverse, adjacency):
    gap = jump(gap_loads.astype(jnp.float32), adjacency)
    multipliers = jnp.zeros_like(gap)
    residual = gap
    direction = gap
    norm_now = jnp.sum(residual * residual, axis=(0, 1))
    for iteration in range(ITERS):
        applied = apply_operator(direction, flexibility, corner_coupling, corner_ids, coarse_inverse, adjacency)
        step_size = norm_now / jnp.sum(direction * applied, axis=(0, 1))
        multipliers = multipliers + step_size * direction
        residual = residual - step_size * applied
        norm_next = jnp.sum(residual * residual, axis=(0, 1))
        direction = residual + (norm_next / norm_now) * direction
        norm_now = norm_next
    return multipliers, residual
```

```python
import jax
import jax.numpy as jnp
from jax import lax
from jax.experimental import pallas as pl
from jax.experimental.pallas import tpu as pltpu
from jax.sharding import PartitionSpec as P

ITERS = 3
FACES = 4
NF = 512
NI = 2048
NC = 16
LOADS = 128
NCG = 1024
BLK = 128
ROWS = BLK + 8
FACE_ORDER = (2, 1, 3, 0)
ARRIVAL = (0, 3, 1, 2)
MESH = pl.DeviceIdType.MESH
F32 = jnp.float32
BF16 = jnp.bfloat16


def flip(index, mask):
    result = index
    bit = 1
    while bit <= mask:
        if mask & bit:
            result = result + bit * (1 - 2 * lax.rem(lax.div(index, bit), 2))
        bit *= 2
    return result


def dot(a, b):
    return jnp.dot(a, b, preferred_element_type=F32)


def sum_rows(gamma, delta):
    row = lax.broadcasted_iota(jnp.int32, (8, LOADS), 0)
    return jnp.where(row == 0, gamma, jnp.where(row == 1, delta, 0.0))


def pick_row(tile, index):
    row = lax.broadcasted_iota(jnp.int32, (8, LOADS), 0)
    return jnp.sum(jnp.where(row == index, tile, 0.0), axis=0, keepdims=True)


def halves(value):
    high = value.astype(BF16)
    return high, (value - high.astype(F32)).astype(BF16)


def kernel(
    adj_ref, ids_ref, cinv_ref, bc_ref, gap_hbm, flex_hbm,
    mult_hbm, res_hbm,
    fv, gapv, rv, pv, uv, xv, frv, rb, frecv, fsend,
    cg, cex, oh, oht, bct, idrecv, brecv,
    s1s, s1r, s2, s3, s4, rb2, yb, cv,
    load_sem, send0, recv0, sendf, recvf, send1, recv1, send2, recv2, send3, recv3, send4, recv4,
):
    me = lax.axis_index("sub")
    core = lax.rem(me, 2)
    yi = lax.rem(lax.div(me, 2), 4)
    zi = lax.rem(lax.div(me, 8), 4)
    xi = lax.div(me, 32)
    chip = lax.div(me, 2)
    grp = xi * 2 + core

    def grp_mask(k):
        return (k // 2) * 32 + (k % 2)

    def remote(src, dst, send, recv, mask):
        return pltpu.make_async_remote_copy(
            src_ref=src, dst_ref=dst, send_sem=send, recv_sem=recv,
            device_id=(flip(me, mask),), device_id_type=MESH,
        )

    barrier = pltpu.get_barrier_semaphore()
    masks = [grp_mask(k) for k in range(1, 8)] + [8, 16, 24, 2, 4, 6]
    for mask in masks:
        pl.semaphore_signal(barrier, inc=1, device_id=(flip(me, mask),), device_id_type=MESH)
    pl.semaphore_wait(barrier, len(masks))

    def gap_copy(f):
        return remote(gap_hbm.at[:, pl.ds(f * NF, NF), :], frecv.at[0, f], sendf.at[0, f], recvf.at[0, f], 1 << f)

    for f in FACE_ORDER:
        gap_copy(f).start()
    gap_load = pltpu.make_async_copy(gap_hbm, gapv, load_sem.at[8])
    gap_load.start()

    setup = []
    core_copy = remote(cinv_ref, cex, send0.at[0], recv0.at[0], 1)
    core_copy.start()
    for f in range(FACES):
        id_copy = remote(ids_ref, idrecv.at[f], send0.at[1 + f], recv0.at[1 + f], 1 << f)
        b_copy = remote(
            bc_ref.at[:, :, pl.ds(f * NF, NF)], brecv.at[f], send0.at[5 + f], recv0.at[5 + f], 1 << f
        )
        id_copy.start()
        b_copy.start()
        setup.append((id_copy, b_copy))

    flex_loads = []
    for s in range(2):
        for f in range(FACES):
            load = pltpu.make_async_copy(
                flex_hbm.at[s, pl.ds(f * NF, NF)], fv.at[s, pl.ds(f * NF, NF)], load_sem.at[s * FACES + f]
            )
            load.start()
            flex_loads.append(load)

    def c_rows(rows, count):
        return cg.at[core, pl.ds(pl.multiple_of(rows, 16), count)]

    def c_stage(base, rows, count, unit):
        part = c_rows(rows, count)
        return [remote(part, part, send0.at[base + k], recv0.at[base + k], unit * k) for k in range(1, 4)]

    core_copy.wait_recv()
    own = cinv_ref[...]
    other = cex[...]
    even = jnp.where(core == 0, own, other)
    odd = jnp.where(core == 0, other, own)
    both = jnp.concatenate([even, odd], axis=0)
    half = jnp.where(core == 0, both[:, : NCG // 2], both[:, NCG // 2 :])
    c_rows(chip * 16, 16)[...] = half.astype(BF16)
    stage_y = c_stage(8, chip * 16, 16, 2)
    for copy in stage_y:
        copy.start()

    lane = lax.broadcasted_iota(jnp.int32, (NC, LOADS), 1)

    def one_hot(ids):
        return [jnp.where(ids == lane + b * LOADS, 1.0, 0.0).astype(F32) for b in range(NCG // LOADS)]

    zeros64 = jnp.zeros((64, LOADS), F32)
    hots = [one_hot(ids_ref[s]) for s in range(2)]
    for b in range(NCG // LOADS):
        tile = jnp.concatenate([hots[0][b], hots[1][b]], axis=0)
        oh[0:32, b * LOADS : (b + 1) * LOADS] = tile.astype(BF16)
        oht[b * LOADS : (b + 1) * LOADS, :] = jnp.concatenate([tile, tile, zeros64], axis=0).T.astype(BF16)

    for copy in stage_y:
        copy.wait_recv()
    stage_z = c_stage(12, lax.div(chip, 4) * 64, 64, 8)
    for copy in stage_z:
        copy.start()

    flags = [[lax.rem(adj_ref[s, f], 2) == 1 for f in range(FACES)] for s in range(2)]
    for f in range(FACES):
        id_copy, b_copy = setup[f]
        id_copy.wait_recv()
        hots = [one_hot(idrecv[f, s]) for s in range(2)]
        for b in range(NCG // LOADS):
            tile = jnp.concatenate([hots[0][b], hots[1][b]], axis=0)
            oh[32 + 32 * f : 64 + 32 * f, b * LOADS : (b + 1) * LOADS] = tile.astype(BF16)
        b_copy.wait_recv()
        for s in range(2):
            for q in range(NF // LOADS):
                cols = slice(q * LOADS, (q + 1) * LOADS)
                mine = bc_ref[s, :, f * NF + q * LOADS : f * NF + (q + 1) * LOADS].astype(F32)
                theirs = jnp.where(flags[s][f], brecv[f, 1, :, cols].astype(F32), brecv[f, 0, :, cols].astype(F32))
                tile = jnp.concatenate([mine, -theirs, mine, -theirs, zeros64], axis=0)
                bct[s, f, cols, :] = tile.T.astype(BF16)

    for copy in stage_z:
        copy.wait_recv()
    stage_x = c_stage(16, xi * 256, 256, 32)
    for copy in stage_x:
        copy.start()
    whole_c = cg.at[core]
    sibling = remote(whole_c, whole_c, send0.at[20], recv0.at[20], 1)

    def clear(i, carry):
        rows = pl.ds(pl.multiple_of(i * 64, 64), 64)
        for s in range(2):
            for ref in (pv, uv, xv):
                ref[s, rows, :] = jnp.zeros((64, LOADS), F32)
        return carry

    lax.fori_loop(0, NI // 64, clear, 0)

    gap_load.wait()
    for f in ARRIVAL:
        gap_copy(f).wait_recv()
        for s in range(2):

            def first(i, carry, s=s, f=f):
                rows = pl.ds(pl.multiple_of(f * NF + i * 128, 128), 128)
                here = pl.ds(pl.multiple_of(i * 128, 128), 128)
                mine = gapv[s, rows, :].astype(F32)
                theirs = jnp.where(
                    flags[s][f], frecv[0, f, 1, here, :].astype(F32), frecv[0, f, 0, here, :].astype(F32)
                )
                value = mine - theirs
                rv[s, rows, :] = value
                rb[s, rows, :] = value.astype(BF16)
                return carry

            lax.fori_loop(0, NF // 128, first, 0)
    for load in flex_loads:
        load.wait()

    def face_copy(k, f):
        return remote(fsend.at[k, f], frecv.at[k + 1, f], sendf.at[k + 1, f], recvf.at[k + 1, f], 1 << f)

    def s1_copy(k, m):
        return remote(
            s1s.at[k, flip_group(m)], s1r.at[k, grp], send1.at[k, m], recv1.at[k, m], grp_mask(m)
        )

    def flip_group(m):
        return flip(grp, m)

    def s2_copy(k, m):
        return remote(s2.at[k, zi], s2.at[k, zi], send2.at[k, m], recv2.at[k, m], 8 * m)

    def s3_copy(k, m):
        return remote(s3.at[k, yi], s3.at[k, yi], send3.at[k, m], recv3.at[k, m], 2 * m)

    def s4_copy(k, m):
        return remote(s4.at[k, grp], s4.at[k, grp], send4.at[k, m], recv4.at[k, m], grp_mask(m))

    zeros64b = jnp.zeros((64, LOADS), BF16)

    def add_slots(ref, k, count):
        total = ref[k, 0].astype(F32)
        for i in range(1, count):
            total = total + ref[k, i].astype(F32)
        return total

    def iteration(k, carry):
        gamma_prev, alpha_prev = carry

        terms = [halves(dot(bc_ref[s], rb[s])) for s in range(2)]
        parts = [terms[0][0], terms[1][0], terms[0][1], terms[1][1], zeros64b]
        dense = dot(oht[...], jnp.concatenate(parts, axis=0))
        s1s[k] = dense.astype(BF16).reshape(8, BLK, LOADS)
        for m in range(1, 8):
            s1_copy(k, m).start()
        s1r[k, grp] = s1s[k, grp]

        gamma = jnp.zeros((1, LOADS), F32)
        delta = jnp.zeros((1, LOADS), F32)
        for f in FACE_ORDER:
            for s in range(2):
                rows = slice(f * NF, (f + 1) * NF)
                frv[s, rows, :] = dot(fv[s, rows, :], rb[s])

                def dots(i, sums, s=s, f=f):
                    at = pl.ds(pl.multiple_of(f * NF + i * 128, 128), 128)
                    fr = frv[s, at, :]
                    r = rv[s, at, :]
                    fsend[k, f, s, pl.ds(pl.multiple_of(i * 128, 128), 128), :] = fr.astype(BF16)
                    g, d = sums
                    return (
                        g + jnp.sum((r * r).reshape(16, 8, LOADS), axis=0),
                        d + jnp.sum((r * fr).reshape(16, 8, LOADS), axis=0),
                    )

                g8, d8 = lax.fori_loop(
                    0, NF // 128, dots, (jnp.zeros((8, LOADS), F32), jnp.zeros((8, LOADS), F32))
                )
                gamma = gamma + jnp.sum(g8, axis=0, keepdims=True)
                delta = delta + jnp.sum(d8, axis=0, keepdims=True)
            face_copy(k, f).start()

        for m in range(1, 8):
            s1_copy(k, m).wait_recv()
        s2[k, zi, :BLK, :] = add_slots(s1r, k, 8)
        s2[k, zi, BLK:, :] = sum_rows(gamma, delta)
        for m in range(1, 4):
            s2_copy(k, m).start()

        @pl.when(k == 0)
        def _():
            for copy in stage_x:
                copy.wait_recv()
            sibling.start()

        for m in range(1, 4):
            s2_copy(k, m).wait_recv()
        s3[k, yi] = add_slots(s2, k, 4)
        for m in range(1, 4):
            s3_copy(k, m).start()
        for m in range(1, 4):
            s3_copy(k, m).wait_recv()
        s4[k, grp] = add_slots(s3, k, 4)
        for m in range(1, 8):
            s4_copy(k, m).start()

        @pl.when(k == 0)
        def _():
            sibling.wait_recv()

        for m in range(1, 8):
            s4_copy(k, m).wait_recv()

        for j in range(8):
            rows = slice(j * BLK, (j + 1) * BLK)
            high, low = halves(s4[k, j, :BLK, :])
            rb2[rows, :LOADS] = high
            rb2[rows, LOADS:] = low
        quad = jnp.zeros((1, LOADS), F32)
        for j in range(8):
            rows = slice(j * BLK, (j + 1) * BLK)
            y = dot(cg[0, rows, :], rb2[: NCG // 2, :]) + dot(cg[1, rows, :], rb2[NCG // 2 :, :])
            y = y[:, :LOADS] + y[:, LOADS:]
            quad = quad + jnp.sum(y * s4[k, j, :BLK, :], axis=0, keepdims=True)
            high, low = halves(y)
            yb[rows, :LOADS] = high
            yb[rows, LOADS:] = low
        tile = s4[k, 0, BLK:, :]
        for j in range(1, 8):
            tile = tile + s4[k, j, BLK:, :]
        gamma = pick_row(tile, 0)
        delta = pick_row(tile, 1)
        picked = dot(oh[...], yb[...])
        cv[...] = picked[:, :LOADS] + picked[:, LOADS:]

        beta = jnp.where(k > 0, gamma / gamma_prev, 0.0)
        alpha = gamma / (2.0 * (delta + quad) - jnp.where(k > 0, beta * gamma / alpha_prev, 0.0))

        for f in ARRIVAL:
            face_copy(k, f).wait_recv()
            for s in range(2):
                theirs = jnp.where(
                    flags[s][f],
                    cv[32 + 32 * f + 16 : 64 + 32 * f, :],
                    cv[32 + 32 * f : 48 + 32 * f, :],
                )
                mine_high, mine_low = halves(cv[16 * s : 16 * s + 16, :])
                high, low = halves(theirs)
                cc = jnp.concatenate([mine_high, high, mine_low, low, zeros64b], axis=0)

                def update(i, carry, s=s, f=f, cc=cc):
                    rows = pl.ds(pl.multiple_of(f * NF + i * 128, 128), 128)
                    here = pl.ds(pl.multiple_of(i * 128, 128), 128)
                    coarse = dot(bct[s, f, here, :], cc)
                    received = jnp.where(
                        flags[s][f],
                        frecv[k + 1, f, 1, here, :].astype(F32),
                        frecv[k + 1, f, 0, here, :].astype(F32),
                    )
                    u = frv[s, rows, :] - received + coarse + beta * uv[s, rows, :]
                    uv[s, rows, :] = u
                    r = rv[s, rows, :]
                    p = r + beta * pv[s, rows, :]
                    pv[s, rows, :] = p
                    xv[s, rows, :] = xv[s, rows, :] + alpha * p
                    r = r - alpha * u
                    rv[s, rows, :] = r
                    rb[s, rows, :] = r.astype(BF16)
                    return carry

                lax.fori_loop(0, NF // 128, update, 0)

        for f in range(FACES):
            face_copy(k, f).wait_send()
        for m in range(1, 8):
            s1_copy(k, m).wait_send()
            s4_copy(k, m).wait_send()
        for m in range(1, 4):
            s2_copy(k, m).wait_send()
            s3_copy(k, m).wait_send()
        return gamma, alpha

    ones = jnp.ones((1, LOADS), F32)
    lax.fori_loop(0, ITERS, iteration, (ones, ones))

    out_mult = pltpu.make_async_copy(xv, mult_hbm, load_sem.at[9])
    out_res = pltpu.make_async_copy(rv, res_hbm, load_sem.at[10])
    out_mult.start()
    out_res.start()
    for f in range(FACES):
        gap_copy(f).wait_send()
        setup[f][0].wait_send()
        setup[f][1].wait_send()
    core_copy.wait_send()
    sibling.wait_send()
    for copy in stage_y + stage_z + stage_x:
        copy.wait_send()
    out_mult.wait()
    out_res.wait()


def shards(gap_loads, flexibility, corner_coupling, corner_ids, coarse_inverse, adjacency):
    ids = jnp.broadcast_to(corner_ids[:, :, None], corner_ids.shape + (LOADS,))
    field = jax.ShapeDtypeStruct((2, NI, LOADS), F32)
    vmem = pl.BlockSpec(memory_space=pltpu.VMEM)
    hbm = pl.BlockSpec(memory_space=pl.ANY)
    dma = pltpu.SemaphoreType.DMA
    return pl.pallas_call(
        kernel,
        out_shape=(field, field),
        in_specs=[pl.BlockSpec(memory_space=pltpu.SMEM), vmem, vmem, vmem, hbm, hbm],
        out_specs=(hbm, hbm),
        scratch_shapes=[
            pltpu.VMEM((2, NI, NI), BF16),
            pltpu.VMEM((2, NI, LOADS), BF16),
            pltpu.VMEM((2, NI, LOADS), F32),
            pltpu.VMEM((2, NI, LOADS), F32),
            pltpu.VMEM((2, NI, LOADS), F32),
            pltpu.VMEM((2, NI, LOADS), F32),
            pltpu.VMEM((2, NI, LOADS), F32),
            pltpu.VMEM((2, NI, LOADS), BF16),
            pltpu.VMEM((ITERS + 1, FACES, 2, NF, LOADS), BF16),
            pltpu.VMEM((ITERS, FACES, 2, NF, LOADS), BF16),
            pltpu.VMEM((2, NCG, NCG // 2), BF16),
            pltpu.VMEM((8, NCG), F32),
            pltpu.VMEM((160, NCG), BF16),
            pltpu.VMEM((NCG, LOADS), BF16),
            pltpu.VMEM((2, FACES, NF, LOADS), BF16),
            pltpu.VMEM((FACES, 2, NC, LOADS), jnp.int32),
            pltpu.VMEM((FACES, 2, NC, NF), BF16),
            pltpu.VMEM((ITERS, 8, BLK, LOADS), BF16),
            pltpu.VMEM((ITERS, 8, BLK, LOADS), BF16),
            pltpu.VMEM((ITERS, 4, ROWS, LOADS), F32),
            pltpu.VMEM((ITERS, 4, ROWS, LOADS), F32),
            pltpu.VMEM((ITERS, 8, ROWS, LOADS), F32),
            pltpu.VMEM((NCG, 2 * LOADS), BF16),
            pltpu.VMEM((NCG, 2 * LOADS), BF16),
            pltpu.VMEM((160, LOADS), F32),
            dma((12,)),
            dma((21,)),
            dma((21,)),
            dma((ITERS + 1, FACES)),
            dma((ITERS + 1, FACES)),
            dma((ITERS, 8)),
            dma((ITERS, 8)),
            dma((ITERS, 4)),
            dma((ITERS, 4)),
            dma((ITERS, 4)),
            dma((ITERS, 4)),
            dma((ITERS, 8)),
            dma((ITERS, 8)),
        ],
        compiler_params=pltpu.CompilerParams(
            collective_id=0, has_side_effects=True, vmem_limit_bytes=60 * 1024 * 1024
        ),
    )(adjacency, ids, coarse_inverse, corner_coupling, gap_loads, flexibility)


def solution(mesh):
    return jax.shard_map(
        shards,
        mesh=mesh,
        in_specs=(
            P("sub", None, None),
            P("sub", None, None),
            P("sub", None, None),
            P("sub", None),
            P("sub", None),
            P("sub", None),
        ),
        out_specs=(P("sub", None, None), P("sub", None, None)),
        check_vma=False,
    )
```

```python
import jax
import jax.numpy as jnp
from jax import lax
from jax.experimental import pallas as pl
from jax.experimental.pallas import tpu as pltpu
from jax.sharding import PartitionSpec as P

ITERS = 3
FACES = 4
NF = 512
NI = 2048
NC = 16
LOADS = 128
NCG = 1024
BLK = 128
ROWS = BLK + 8
HALF = NCG // 2
WIDE = HALF + LOADS
FACE_ORDER = (2, 1, 3, 0)
ARRIVAL = (0, 3, 1, 2)
MESH = pl.DeviceIdType.MESH
F32 = jnp.float32
BF16 = jnp.bfloat16


def flip(index, mask):
    result = index
    bit = 1
    while bit <= mask:
        if mask & bit:
            result = result + bit * (1 - 2 * lax.rem(lax.div(index, bit), 2))
        bit *= 2
    return result


def dot(a, b):
    return jnp.dot(a, b, preferred_element_type=F32)


def sum_rows(gamma, delta):
    row = lax.broadcasted_iota(jnp.int32, (8, LOADS), 0)
    return jnp.where(row == 0, gamma, jnp.where(row == 1, delta, 0.0))


def pick_row(tile, index):
    row = lax.broadcasted_iota(jnp.int32, (8, LOADS), 0)
    return jnp.sum(jnp.where(row == index, tile, 0.0), axis=0, keepdims=True)


def halves(value):
    high = value.astype(BF16)
    return high, (value - high.astype(F32)).astype(BF16)


def kernel(
    adj_ref, ids_ref, cinv_ref, bc_ref, gap_hbm, flex_hbm,
    mult_hbm, res_hbm,
    fv, gapv, rv, pv, uv, xv, frv, rb, frecv, fsend,
    cg, cex, oh, oht, bct, idrecv, brecv,
    s1s, s1r, a1, a2, b1, b2, d1, d2, s4, rb2, yb, cv,
    load_sem, send0, recv0, sendg, recvg, sendf, recvf, send1, recv1,
    senda1, recva1, senda2, recva2, sendb1, recvb1, sendb2, recvb2,
    sendd1, recvd1, sendd2, recvd2, send4, recv4,
):
    me = lax.axis_index("sub")
    core = lax.rem(me, 2)
    zi = lax.rem(lax.div(me, 8), 4)
    xi = lax.div(me, 32)
    chip = lax.div(me, 2)
    grp = lax.rem(me, 8)

    def remote(src, dst, send, recv, mask):
        return pltpu.make_async_remote_copy(
            src_ref=src, dst_ref=dst, send_sem=send, recv_sem=recv,
            device_id=(flip(me, mask),), device_id_type=MESH,
        )

    barrier = pltpu.get_barrier_semaphore()
    masks = [1, 2, 3, 4, 5, 6, 7, 8, 16, 24, 32, 64, 96]
    for mask in masks:
        pl.semaphore_signal(barrier, inc=1, device_id=(flip(me, mask),), device_id_type=MESH)
    pl.semaphore_wait(barrier, len(masks))

    def gap_copy(f, s):
        at = 2 * f + s
        return remote(
            gap_hbm.at[s, pl.ds(f * NF, NF), :], frecv.at[0, f, s], sendg.at[at], recvg.at[at], 1 << f
        )

    core_copy = remote(cinv_ref, cex, send0.at[0], recv0.at[0], 1)
    core_copy.start()
    gap_copy(2, 0).start()
    gap_copy(1, 0).start()
    gap_load = pltpu.make_async_copy(gap_hbm, gapv, load_sem.at[8])
    gap_load.start()

    setup = []
    for f in range(FACES):
        id_copy = remote(ids_ref, idrecv.at[f], send0.at[1 + f], recv0.at[1 + f], 1 << f)
        b_copy = remote(
            bc_ref.at[:, :, pl.ds(f * NF, NF)], brecv.at[f], send0.at[5 + f], recv0.at[5 + f], 1 << f
        )
        setup.append((id_copy, b_copy))

    flex_loads = []
    for s in range(2):
        for f in range(FACES):
            load = pltpu.make_async_copy(
                flex_hbm.at[s, pl.ds(f * NF, NF)], fv.at[s, pl.ds(f * NF, NF)], load_sem.at[s * FACES + f]
            )
            load.start()
            flex_loads.append(load)

    def c_rows(rows, count):
        return cg.at[core, pl.ds(pl.multiple_of(rows, 16), count)]

    def c_stage(base, rows, count, unit):
        part = c_rows(rows, count)
        return [remote(part, part, send0.at[base + k], recv0.at[base + k], unit * k) for k in range(1, 4)]

    core_copy.wait_recv()
    own = cinv_ref[...]
    other = cex[...]
    even = jnp.where(core == 0, own, other)
    odd = jnp.where(core == 0, other, own)
    both = jnp.concatenate([even, odd], axis=0)
    half = jnp.where(core == 0, both[:, :HALF], both[:, HALF:])
    across = lax.broadcasted_iota(jnp.int32, (16, NCG), 1)
    down = lax.broadcasted_iota(jnp.int32, (16, NCG), 0)
    rest = both - both.astype(BF16).astype(F32)
    rest = jnp.sum(jnp.where(across == down + chip * 16, rest, 0.0), axis=1, keepdims=True)
    packed = jnp.concatenate([half, jnp.broadcast_to(rest, (16, LOADS))], axis=1)
    c_rows(chip * 16, 16)[...] = packed.astype(BF16)
    stage_y = c_stage(8, chip * 16, 16, 2)
    for copy in stage_y:
        copy.start()
    for f, s in ((2, 1), (1, 1), (3, 0), (3, 1), (0, 0), (0, 1)):
        gap_copy(f, s).start()
    for id_copy, b_copy in setup:
        id_copy.start()
        b_copy.start()

    lane = lax.broadcasted_iota(jnp.int32, (NC, LOADS), 1)

    def one_hot(ids):
        return [jnp.where(ids == lane + b * LOADS, 1.0, 0.0).astype(F32) for b in range(NCG // LOADS)]

    zeros64 = jnp.zeros((64, LOADS), F32)
    hots = [one_hot(ids_ref[s]) for s in range(2)]
    for b in range(NCG // LOADS):
        tile = jnp.concatenate([hots[0][b], hots[1][b]], axis=0)
        oh[0:32, b * LOADS : (b + 1) * LOADS] = tile.astype(BF16)
        oht[b * LOADS : (b + 1) * LOADS, :] = jnp.concatenate([tile, tile, zeros64], axis=0).T.astype(BF16)

    for copy in stage_y:
        copy.wait_recv()
    stage_z = c_stage(12, lax.div(chip, 4) * 64, 64, 8)
    for copy in stage_z:
        copy.start()

    flags = [[lax.rem(adj_ref[s, f], 2) == 1 for f in range(FACES)] for s in range(2)]
    for f in range(FACES):
        id_copy, b_copy = setup[f]
        id_copy.wait_recv()
        hots = [one_hot(idrecv[f, s]) for s in range(2)]
        for b in range(NCG // LOADS):
            tile = jnp.concatenate([hots[0][b], hots[1][b]], axis=0)
            oh[32 + 32 * f : 64 + 32 * f, b * LOADS : (b + 1) * LOADS] = tile.astype(BF16)
        b_copy.wait_recv()
        for s in range(2):
            for q in range(NF // LOADS):
                cols = slice(q * LOADS, (q + 1) * LOADS)
                mine = bc_ref[s, :, f * NF + q * LOADS : f * NF + (q + 1) * LOADS].astype(F32)
                theirs = jnp.where(flags[s][f], brecv[f, 1, :, cols].astype(F32), brecv[f, 0, :, cols].astype(F32))
                tile = jnp.concatenate([mine, -theirs, mine, -theirs, zeros64], axis=0)
                bct[s, f, cols, :] = tile.T.astype(BF16)

    for copy in stage_z:
        copy.wait_recv()
    stage_x = c_stage(16, xi * 256, 256, 32)
    for copy in stage_x:
        copy.start()
    whole_c = cg.at[core]
    sibling = remote(whole_c, whole_c, send0.at[20], recv0.at[20], 1)

    def clear(i, carry):
        rows = pl.ds(pl.multiple_of(i * 64, 64), 64)
        for s in range(2):
            for ref in (pv, uv, xv):
                ref[s, rows, :] = jnp.zeros((64, LOADS), F32)
        return carry

    lax.fori_loop(0, NI // 64, clear, 0)

    gap_load.wait()
    for f in ARRIVAL:
        gap_copy(f, 0).wait_recv()
        gap_copy(f, 1).wait_recv()
        for s in range(2):
            for i in range(NF // 128):
                rows = slice(f * NF + i * 128, f * NF + i * 128 + 128)
                here = slice(i * 128, i * 128 + 128)
                mine = gapv[s, rows, :].astype(F32)
                theirs = jnp.where(
                    flags[s][f], frecv[0, f, 1, here, :].astype(F32), frecv[0, f, 0, here, :].astype(F32)
                )
                value = mine - theirs
                rv[0, s, rows, :] = value
                rb[s, rows, :] = value.astype(BF16)
    for load in flex_loads:
        load.wait()

    def face_copy(k, f):
        return remote(fsend.at[k, f], frecv.at[k + 1, f], sendf.at[k + 1, f], recvf.at[k + 1, f], 1 << f)

    def s1_copy(k, m):
        return remote(
            s1s.at[k, flip_group(m)], s1r.at[k, grp], send1.at[k, m], recv1.at[k, m], m
        )

    def flip_group(m):
        return flip(grp, m)

    def a1_copy(k, m):
        return remote(a1.at[k, zi], a1.at[k, zi], senda1.at[k, m], recva1.at[k, m], 8 * m)

    def a2_copy(k, m):
        return remote(a2.at[k, xi], a2.at[k, xi], senda2.at[k, m], recva2.at[k, m], 32 * m)

    def b1_copy(k, m):
        return remote(b1.at[k, xi], b1.at[k, xi], sendb1.at[k, m], recvb1.at[k, m], 32 * m)

    def b2_copy(k, m):
        return remote(b2.at[k, zi], b2.at[k, zi], sendb2.at[k, m], recvb2.at[k, m], 8 * m)

    def d1_copy(k, m):
        return remote(d1.at[k, zi], d1.at[k, zi], sendd1.at[k, m], recvd1.at[k, m], 8 * m)

    def d2_copy(k, m):
        return remote(d2.at[k, xi], d2.at[k, xi], sendd2.at[k, m], recvd2.at[k, m], 32 * m)

    def y4_copy(k, m):
        return remote(s4.at[k, grp], s4.at[k, grp], send4.at[k, m], recv4.at[k, m], 2 * m)

    def c4_copy(k, m):
        block = s4.at[k, flip(grp, 2 * m)]
        return remote(block, block, send4.at[k, 4 + m], recv4.at[k, 4 + m], 1)

    zeros64b = jnp.zeros((64, LOADS), BF16)

    def add_slots(ref, k, count):
        total = ref[k, 0].astype(F32)
        for i in range(1, count):
            total = total + ref[k, i].astype(F32)
        return total

    def follow(k, beta, alpha):
        for s in range(2):
            for i in range(NI // 128):
                rows = slice(i * 128, i * 128 + 128)
                p = rv[k, s, rows, :] + beta * pv[s, rows, :]
                pv[s, rows, :] = p
                xv[s, rows, :] = xv[s, rows, :] + alpha * p

    def iteration(k, carry):
        gamma_prev, alpha_prev, beta_prev = carry

        terms = [halves(dot(bc_ref[s], rb[s])) for s in range(2)]
        parts = [terms[0][0], terms[1][0], terms[0][1], terms[1][1], zeros64b]
        s1s[k] = dot(oht[...], jnp.concatenate(parts, axis=0)).astype(BF16).reshape(8, BLK, LOADS)
        for m in range(1, 8):
            s1_copy(k, m).start()
        s1r[k, grp] = s1s[k, grp]

        gamma = jnp.zeros((8, LOADS), F32)
        delta = jnp.zeros((8, LOADS), F32)
        for place, f in enumerate(FACE_ORDER):
            for s in range(2):
                frv[s, f * NF : (f + 1) * NF, :] = dot(fv[s, f * NF : (f + 1) * NF, :], rb[s])
                for i in range(NF // 128):
                    rows = slice(f * NF + i * 128, f * NF + i * 128 + 128)
                    fr = frv[s, rows, :]
                    r = rv[k, s, rows, :]
                    fsend[k, f, s, i * 128 : i * 128 + 128, :] = fr.astype(BF16)
                    gamma = gamma + jnp.sum((r * r).reshape(16, 8, LOADS), axis=0)
                    delta = delta + jnp.sum((r * fr).reshape(16, 8, LOADS), axis=0)
            if f != 3:
                face_copy(k, f).start()
            if place == 1:
                for m in range(1, 8):
                    s1_copy(k, m).wait_recv()
                total = add_slots(s1r, k, 8)
                a1[k, zi] = total[:64]
                b1[k, xi] = total[64:]
                for m in range(1, 4):
                    a1_copy(k, m).start()
                    b1_copy(k, m).start()
        d1[k, zi] = sum_rows(
            jnp.sum(gamma, axis=0, keepdims=True), jnp.sum(delta, axis=0, keepdims=True)
        )
        for m in range(1, 4):
            d1_copy(k, m).start()

        for m in range(1, 4):
            a1_copy(k, m).wait_recv()
            b1_copy(k, m).wait_recv()
        a2[k, xi] = add_slots(a1, k, 4)
        b2[k, zi] = add_slots(b1, k, 4)
        for m in range(1, 4):
            a2_copy(k, m).start()
            b2_copy(k, m).start()
        face_copy(k, 3).start()
        for m in range(1, 4):
            d1_copy(k, m).wait_recv()
        d2[k, xi] = add_slots(d1, k, 4)
        for m in range(1, 4):
            d2_copy(k, m).start()

        @pl.when(k > 0)
        def _():
            follow(k - 1, beta_prev, alpha_prev)

        for m in range(1, 4):
            a2_copy(k, m).wait_recv()
            b2_copy(k, m).wait_recv()
            d2_copy(k, m).wait_recv()
        s4[k, grp, :64, :] = add_slots(a2, k, 4)
        s4[k, grp, 64:BLK, :] = add_slots(b2, k, 4)
        s4[k, grp, BLK:, :] = add_slots(d2, k, 4)
        for m in range(1, 4):
            y4_copy(k, m).start()
        c4_copy(k, 0).start()

        @pl.when(k == 0)
        def _():
            for copy in stage_x:
                copy.wait_recv()
            sibling.start()

        for f in ARRIVAL:
            face_copy(k, f).wait_recv()
            for s in range(2):
                for i in range(NF // 128):
                    rows = slice(f * NF + i * 128, f * NF + i * 128 + 128)
                    here = slice(i * 128, i * 128 + 128)
                    received = jnp.where(
                        flags[s][f],
                        frecv[k + 1, f, 1, here, :].astype(F32),
                        frecv[k + 1, f, 0, here, :].astype(F32),
                    )
                    frv[s, rows, :] = frv[s, rows, :] - received

        for m in range(1, 4):
            y4_copy(k, m).wait_recv()
            c4_copy(k, m).start()

        @pl.when(k == 0)
        def _():
            sibling.wait_recv()

        for m in range(4):
            c4_copy(k, m).wait_recv()

        for j in range(8):
            rows = slice(j * BLK, (j + 1) * BLK)
            high, low = halves(s4[k, j, :BLK, :])
            rb2[rows, :LOADS] = high
            rb2[rows, LOADS:] = low
        quad = jnp.zeros((8, LOADS), F32)
        for j in range(8):
            rows = slice(j * BLK, (j + 1) * BLK)
            rhs = s4[k, j, :BLK, :]
            y = dot(cg[0, rows, :HALF], rb2[:HALF, :]) + dot(cg[1, rows, :HALF], rb2[HALF:, :])
            y = y[:, :LOADS] + y[:, LOADS:] + cg[0, rows, HALF:].astype(F32) * rhs
            quad = quad + jnp.sum((y * rhs).reshape(16, 8, LOADS), axis=0)
            high, low = halves(y)
            yb[rows, :LOADS] = high
            yb[rows, LOADS:] = low
        quad = jnp.sum(quad, axis=0, keepdims=True)
        tile = s4[k, 0, BLK:, :]
        for j in range(1, 8):
            tile = tile + s4[k, j, BLK:, :]
        gamma = pick_row(tile, 0)
        delta = pick_row(tile, 1)
        picked = dot(oh[...], yb[...])
        cv[...] = picked[:, :LOADS] + picked[:, LOADS:]

        beta = jnp.where(k > 0, gamma / gamma_prev, 0.0)
        alpha = gamma / (2.0 * (delta + quad) - jnp.where(k > 0, beta * gamma / alpha_prev, 0.0))

        for f in range(FACES):
            for s in range(2):
                theirs = jnp.where(
                    flags[s][f],
                    cv[32 + 32 * f + 16 : 64 + 32 * f, :],
                    cv[32 + 32 * f : 48 + 32 * f, :],
                )
                mine_high, mine_low = halves(cv[16 * s : 16 * s + 16, :])
                high, low = halves(theirs)
                cc = jnp.concatenate([mine_high, high, mine_low, low, zeros64b], axis=0)
                for i in range(NF // 128):
                    rows = slice(f * NF + i * 128, f * NF + i * 128 + 128)
                    coarse = dot(bct[s, f, i * 128 : i * 128 + 128, :], cc)
                    u = frv[s, rows, :] + coarse + beta * uv[s, rows, :]
                    uv[s, rows, :] = u
                    r = rv[k, s, rows, :] - alpha * u
                    rv[k + 1, s, rows, :] = r
                    rb[s, rows, :] = r.astype(BF16)

        for f in range(FACES):
            face_copy(k, f).wait_send()
            c4_copy(k, f).wait_send()
        for m in range(1, 8):
            s1_copy(k, m).wait_send()
        for m in range(1, 4):
            a1_copy(k, m).wait_send()
            a2_copy(k, m).wait_send()
            b1_copy(k, m).wait_send()
            b2_copy(k, m).wait_send()
            d1_copy(k, m).wait_send()
            d2_copy(k, m).wait_send()
            y4_copy(k, m).wait_send()
        return gamma, alpha, beta

    ones = jnp.ones((1, LOADS), F32)
    _, alpha, beta = lax.fori_loop(0, ITERS, iteration, (ones, ones, ones))

    out_res = pltpu.make_async_copy(rv.at[ITERS], res_hbm, load_sem.at[10])
    out_res.start()
    follow(ITERS - 1, beta, alpha)
    out_mult = pltpu.make_async_copy(xv, mult_hbm, load_sem.at[9])
    out_mult.start()
    for f in range(FACES):
        gap_copy(f, 0).wait_send()
        gap_copy(f, 1).wait_send()
        setup[f][0].wait_send()
        setup[f][1].wait_send()
    core_copy.wait_send()
    sibling.wait_send()
    for copy in stage_y + stage_z + stage_x:
        copy.wait_send()
    out_mult.wait()
    out_res.wait()


def shards(gap_loads, flexibility, corner_coupling, corner_ids, coarse_inverse, adjacency):
    ids = jnp.broadcast_to(corner_ids[:, :, None], corner_ids.shape + (LOADS,))
    field = jax.ShapeDtypeStruct((2, NI, LOADS), F32)
    vmem = pl.BlockSpec(memory_space=pltpu.VMEM)
    hbm = pl.BlockSpec(memory_space=pl.ANY)
    dma = pltpu.SemaphoreType.DMA
    return pl.pallas_call(
        kernel,
        out_shape=(field, field),
        in_specs=[pl.BlockSpec(memory_space=pltpu.SMEM), vmem, vmem, vmem, hbm, hbm],
        out_specs=(hbm, hbm),
        scratch_shapes=[
            pltpu.VMEM((2, NI, NI), BF16),
            pltpu.VMEM((2, NI, LOADS), BF16),
            pltpu.VMEM((ITERS + 1, 2, NI, LOADS), F32),
            pltpu.VMEM((2, NI, LOADS), F32),
            pltpu.VMEM((2, NI, LOADS), F32),
            pltpu.VMEM((2, NI, LOADS), F32),
            pltpu.VMEM((2, NI, LOADS), F32),
            pltpu.VMEM((2, NI, LOADS), BF16),
            pltpu.VMEM((ITERS + 1, FACES, 2, NF, LOADS), BF16),
            pltpu.VMEM((ITERS, FACES, 2, NF, LOADS), BF16),
            pltpu.VMEM((2, NCG, WIDE), BF16),
            pltpu.VMEM((8, NCG), F32),
            pltpu.VMEM((160, NCG), BF16),
            pltpu.VMEM((NCG, LOADS), BF16),
            pltpu.VMEM((2, FACES, NF, LOADS), BF16),
            pltpu.VMEM((FACES, 2, NC, LOADS), jnp.int32),
            pltpu.VMEM((FACES, 2, NC, NF), BF16),
            pltpu.VMEM((ITERS, 8, BLK, LOADS), BF16),
            pltpu.VMEM((ITERS, 8, BLK, LOADS), BF16),
            pltpu.VMEM((ITERS, 4, 64, LOADS), F32),
            pltpu.VMEM((ITERS, 4, 64, LOADS), F32),
            pltpu.VMEM((ITERS, 4, 64, LOADS), F32),
            pltpu.VMEM((ITERS, 4, 64, LOADS), F32),
            pltpu.VMEM((ITERS, 4, 8, LOADS), F32),
            pltpu.VMEM((ITERS, 4, 8, LOADS), F32),
            pltpu.VMEM((ITERS, 8, ROWS, LOADS), F32),
            pltpu.VMEM((NCG, 2 * LOADS), BF16),
            pltpu.VMEM((NCG, 2 * LOADS), BF16),
            pltpu.VMEM((160, LOADS), F32),
            dma((12,)),
            dma((21,)),
            dma((21,)),
            dma((8,)),
            dma((8,)),
            dma((ITERS + 1, FACES)),
            dma((ITERS + 1, FACES)),
            dma((ITERS, 8)),
            dma((ITERS, 8)),
        ]
        + [dma((ITERS, 4))] * 12
        + [dma((ITERS, 8))] * 2,
        compiler_params=pltpu.CompilerParams(
            collective_id=0, has_side_effects=True, vmem_limit_bytes=60 * 1024 * 1024
        ),
    )(adjacency, ids, coarse_inverse, corner_coupling, gap_loads, flexibility)


def solution(mesh):
    return jax.shard_map(
        shards,
        mesh=mesh,
        in_specs=(
            P("sub", None, None),
            P("sub", None, None),
            P("sub", None, None),
            P("sub", None),
            P("sub", None),
            P("sub", None),
        ),
        out_specs=(P("sub", None, None), P("sub", None, None)),
        check_vma=False,
    )
```

```python
import jax
import jax.numpy as jnp
from jax import lax
from jax.experimental import pallas as pl
from jax.experimental.pallas import tpu as pltpu
from jax.sharding import PartitionSpec as P

ITERS = 3
FACES = 4
NF = 512
NI = 2048
NC = 16
LOADS = 128
NCG = 1024
BLK = 128
HALF = NCG // 2
WIDE = HALF + LOADS
FACE_ORDER = (2, 1, 3, 0)
ARRIVAL = (0, 3, 1, 2)
MESH = pl.DeviceIdType.MESH
F32 = jnp.float32
BF16 = jnp.bfloat16


def flip(index, mask):
    result = index
    bit = 1
    while bit <= mask:
        if mask & bit:
            result = result + bit * (1 - 2 * lax.rem(lax.div(index, bit), 2))
        bit *= 2
    return result


def dot(a, b):
    return jnp.dot(a, b, preferred_element_type=F32)


def sum_rows(gamma, delta):
    row = lax.broadcasted_iota(jnp.int32, (8, LOADS), 0)
    return jnp.where(row == 0, gamma, jnp.where(row == 1, delta, 0.0))


def pick_row(tile, index):
    row = lax.broadcasted_iota(jnp.int32, (8, LOADS), 0)
    return jnp.sum(jnp.where(row == index, tile, 0.0), axis=0, keepdims=True)


def halves(value):
    high = value.astype(BF16)
    return high, (value - high.astype(F32)).astype(BF16)


def kernel(
    adj_ref, ids_ref, cinv_ref, bc_ref, gap_hbm, flex_hbm,
    mult_hbm, res_hbm,
    fv, gapv, rv, pv, uv, xv, frv, rb, frecv, fsend,
    cg, cex, oh, scat, bct, idg, idz, brecv,
    s1, a1, a2, b1, b2, d1, d2, d3, s4, rb2, yb, cv,
    load_sem, send0, recv0, sendg, recvg, sendf, recvf, send1, recv1,
    senda1, recva1, senda2, recva2, sendb1, recvb1, sendb2, recvb2,
    sendd1, recvd1, sendd2, recvd2, sendd3, recvd3, send4, recv4, sendi, recvi,
):
    me = lax.axis_index("sub")
    core = lax.rem(me, 2)
    zi = lax.rem(lax.div(me, 8), 4)
    xi = lax.div(me, 32)
    chip = lax.div(me, 2)
    grp = lax.rem(me, 8)

    def remote(src, dst, send, recv, mask):
        return pltpu.make_async_remote_copy(
            src_ref=src, dst_ref=dst, send_sem=send, recv_sem=recv,
            device_id=(flip(me, mask),), device_id_type=MESH,
        )

    barrier = pltpu.get_barrier_semaphore()
    masks = [1, 2, 3, 4, 5, 6, 7, 8, 16, 24, 32, 64, 96]
    for mask in masks:
        pl.semaphore_signal(barrier, inc=1, device_id=(flip(me, mask),), device_id_type=MESH)
    pl.semaphore_wait(barrier, len(masks))

    def gap_copy(f, s):
        at = 2 * f + s
        return remote(
            gap_hbm.at[s, pl.ds(f * NF, NF), :], frecv.at[0, f, s], sendg.at[at], recvg.at[at], 1 << f
        )

    core_copy = remote(cinv_ref, cex, send0.at[0], recv0.at[0], 1)
    core_copy.start()
    gap_copy(2, 0).start()
    gap_copy(1, 0).start()
    gap_load = pltpu.make_async_copy(gap_hbm, gapv, load_sem.at[8])
    gap_load.start()

    id_copies = [
        remote(ids_ref, idg.at[grp], sendi.at[m], recvi.at[m], m) for m in range(1, 8)
    ] + [remote(ids_ref, idz, sendi.at[0], recvi.at[0], 8)]
    b_copies = [
        remote(bc_ref.at[:, :, pl.ds(f * NF, NF)], brecv.at[f], send0.at[5 + f], recv0.at[5 + f], 1 << f)
        for f in range(FACES)
    ]

    flex_loads = []
    for s in range(2):
        for f in range(FACES):
            load = pltpu.make_async_copy(
                flex_hbm.at[s, pl.ds(f * NF, NF)], fv.at[s, pl.ds(f * NF, NF)], load_sem.at[s * FACES + f]
            )
            load.start()
            flex_loads.append(load)

    def c_rows(rows, count):
        return cg.at[core, pl.ds(pl.multiple_of(rows, 16), count)]

    def c_stage(base, rows, count, unit):
        part = c_rows(rows, count)
        return [remote(part, part, send0.at[base + k], recv0.at[base + k], unit * k) for k in range(1, 4)]

    core_copy.wait_recv()
    own = cinv_ref[...]
    other = cex[...]
    even = jnp.where(core == 0, own, other)
    odd = jnp.where(core == 0, other, own)
    both = jnp.concatenate([even, odd], axis=0)
    half = jnp.where(core == 0, both[:, :HALF], both[:, HALF:])
    across = lax.broadcasted_iota(jnp.int32, (16, NCG), 1)
    down = lax.broadcasted_iota(jnp.int32, (16, NCG), 0)
    rest = both - both.astype(BF16).astype(F32)
    rest = jnp.sum(jnp.where(across == down + chip * 16, rest, 0.0), axis=1, keepdims=True)
    packed = jnp.concatenate([half, jnp.broadcast_to(rest, (16, LOADS))], axis=1)
    c_rows(chip * 16, 16)[...] = packed.astype(BF16)
    stage_y = c_stage(8, chip * 16, 16, 2)
    for copy in stage_y:
        copy.start()
    for f, s in ((2, 1), (1, 1), (3, 0), (3, 1), (0, 0), (0, 1)):
        gap_copy(f, s).start()
    for copy in id_copies + b_copies:
        copy.start()
    idg[grp] = ids_ref[...]

    lane = lax.broadcasted_iota(jnp.int32, (NC, LOADS), 1)

    def one_hot(ids):
        return [jnp.where(ids == lane + b * LOADS, 1.0, 0.0).astype(F32) for b in range(NCG // LOADS)]

    zeros64 = jnp.zeros((64, LOADS), F32)
    flags = [[lax.rem(adj_ref[s, f], 2) == 1 for f in range(FACES)] for s in range(2)]

    def spread(base, ids):
        hots = [one_hot(ids[s]) for s in range(2)]
        for b in range(NCG // LOADS):
            tile = jnp.concatenate([hots[0][b], hots[1][b]], axis=0)
            oh[base : base + 32, b * LOADS : (b + 1) * LOADS] = tile.astype(BF16)

    def build_scatter():
        for copy in id_copies:
            copy.wait_recv()
        mine = lane + grp * BLK
        for q in range(2):
            tiles = [
                jnp.where(idg[e, s] == mine, 1.0, 0.0).astype(F32)
                for e in range(4 * q, 4 * q + 4)
                for s in range(2)
            ]
            scat[:, q * LOADS : (q + 1) * LOADS] = jnp.concatenate(tiles, axis=0).T.astype(BF16)

    def build_corners():
        spread(0, ids_ref)
        for f in range(3):
            spread(32 + 32 * f, idg.at[flip(grp, 1 << f)])
        spread(32 + 32 * 3, idz)
        for f in range(FACES):
            b_copies[f].wait_recv()
            for s in range(2):
                for q in range(NF // LOADS):
                    cols = slice(q * LOADS, (q + 1) * LOADS)
                    mine = bc_ref[s, :, f * NF + q * LOADS : f * NF + (q + 1) * LOADS].astype(F32)
                    theirs = jnp.where(
                        flags[s][f], brecv[f, 1, :, cols].astype(F32), brecv[f, 0, :, cols].astype(F32)
                    )
                    tile = jnp.concatenate([mine, -theirs, mine, -theirs, zeros64], axis=0)
                    bct[s, f, cols, :] = tile.T.astype(BF16)

    def clear(i, carry):
        rows = pl.ds(pl.multiple_of(i * 64, 64), 64)
        for s in range(2):
            for ref in (pv, uv, xv):
                ref[s, rows, :] = jnp.zeros((64, LOADS), F32)
        return carry

    lax.fori_loop(0, NI // 64, clear, 0)

    for copy in stage_y:
        copy.wait_recv()
    stage_z = c_stage(12, lax.div(chip, 4) * 64, 64, 8)
    for copy in stage_z:
        copy.start()

    for copy in stage_z:
        copy.wait_recv()
    stage_x = c_stage(16, xi * 256, 256, 32)
    for copy in stage_x:
        copy.start()
    whole_c = cg.at[core]
    sibling = remote(whole_c, whole_c, send0.at[20], recv0.at[20], 1)

    gap_load.wait()
    for f in ARRIVAL:
        gap_copy(f, 0).wait_recv()
        gap_copy(f, 1).wait_recv()
        for s in range(2):
            for i in range(NF // 128):
                rows = slice(f * NF + i * 128, f * NF + i * 128 + 128)
                here = slice(i * 128, i * 128 + 128)
                mine = gapv[s, rows, :].astype(F32)
                theirs = jnp.where(
                    flags[s][f], frecv[0, f, 1, here, :].astype(F32), frecv[0, f, 0, here, :].astype(F32)
                )
                value = mine - theirs
                rv[0, s, rows, :] = value
                rb[s, rows, :] = value.astype(BF16)
    for load in flex_loads:
        load.wait()

    def face_copy(k, f):
        return remote(fsend.at[k, f], frecv.at[k + 1, f], sendf.at[k + 1, f], recvf.at[k + 1, f], 1 << f)

    def s1_copy(k, m):
        return remote(s1.at[k, grp], s1.at[k, grp], send1.at[k, m], recv1.at[k, m], m)

    def d3_copy(k, m):
        return remote(d3.at[k, grp], d3.at[k, grp], sendd3.at[k, m], recvd3.at[k, m], m)

    def a1_copy(k, m):
        return remote(a1.at[k, zi], a1.at[k, zi], senda1.at[k, m], recva1.at[k, m], 8 * m)

    def a2_copy(k, m):
        return remote(a2.at[k, xi], a2.at[k, xi], senda2.at[k, m], recva2.at[k, m], 32 * m)

    def b1_copy(k, m):
        return remote(b1.at[k, xi], b1.at[k, xi], sendb1.at[k, m], recvb1.at[k, m], 32 * m)

    def b2_copy(k, m):
        return remote(b2.at[k, zi], b2.at[k, zi], sendb2.at[k, m], recvb2.at[k, m], 8 * m)

    def d1_copy(k, m):
        return remote(d1.at[k, zi], d1.at[k, zi], sendd1.at[k, m], recvd1.at[k, m], 8 * m)

    def d2_copy(k, m):
        return remote(d2.at[k, xi], d2.at[k, xi], sendd2.at[k, m], recvd2.at[k, m], 32 * m)

    def y4_copy(k, m):
        return remote(s4.at[k, grp], s4.at[k, grp], send4.at[k, m], recv4.at[k, m], 2 * m)

    def c4_copy(k, m):
        block = s4.at[k, flip(grp, 2 * m)]
        return remote(block, block, send4.at[k, 4 + m], recv4.at[k, 4 + m], 1)

    zeros64b = jnp.zeros((64, LOADS), BF16)

    def sent(k):
        for f in range(FACES):
            face_copy(k, f).wait_send()
            c4_copy(k, f).wait_send()
        for m in range(1, 8):
            s1_copy(k, m).wait_send()
            d3_copy(k, m).wait_send()
        for m in range(1, 4):
            for copy in (a1_copy, a2_copy, b1_copy, b2_copy, d1_copy, d2_copy, y4_copy):
                copy(k, m).wait_send()

    def add_slots(ref, k, count):
        total = ref[k, 0].astype(F32)
        for i in range(1, count):
            total = total + ref[k, i].astype(F32)
        return total

    def follow(k, beta, alpha):
        for s in range(2):
            for i in range(NI // 128):
                rows = slice(i * 128, i * 128 + 128)
                p = rv[k, s, rows, :] + beta * pv[s, rows, :]
                pv[s, rows, :] = p
                xv[s, rows, :] = xv[s, rows, :] + alpha * p

    def iteration(k, carry):
        gamma_prev, alpha_prev, beta_prev = carry

        s1[k, grp] = jnp.concatenate([dot(bc_ref[s], rb[s]) for s in range(2)], axis=0).astype(BF16)
        for m in range(1, 8):
            s1_copy(k, m).start()

        gamma = jnp.zeros((8, LOADS), F32)
        delta = jnp.zeros((8, LOADS), F32)
        for place, f in enumerate(FACE_ORDER):
            for s in range(2):
                frv[s, f * NF : (f + 1) * NF, :] = dot(fv[s, f * NF : (f + 1) * NF, :], rb[s])
                for i in range(NF // 128):
                    rows = slice(f * NF + i * 128, f * NF + i * 128 + 128)
                    fr = frv[s, rows, :]
                    r = rv[k, s, rows, :]
                    fsend[k, f, s, i * 128 : i * 128 + 128, :] = fr.astype(BF16)
                    gamma = gamma + jnp.sum((r * r).reshape(16, 8, LOADS), axis=0)
                    delta = delta + jnp.sum((r * fr).reshape(16, 8, LOADS), axis=0)
            if f not in (0, 3):
                face_copy(k, f).start()
            if place == 1:

                @pl.when(k == 0)
                def _():
                    build_scatter()

                for m in range(1, 8):
                    s1_copy(k, m).wait_recv()
                total = dot(scat[...], s1[k].reshape(2 * BLK, LOADS))
                a1[k, zi] = total[:64]
                b1[k, xi] = total[64:]
                for m in range(1, 4):
                    a1_copy(k, m).start()
                    b1_copy(k, m).start()
        d1[k, zi] = sum_rows(
            jnp.sum(gamma, axis=0, keepdims=True), jnp.sum(delta, axis=0, keepdims=True)
        )
        for m in range(1, 4):
            d1_copy(k, m).start()

        for m in range(1, 4):
            a1_copy(k, m).wait_recv()
            b1_copy(k, m).wait_recv()
        a2[k, xi] = add_slots(a1, k, 4)
        b2[k, zi] = add_slots(b1, k, 4)
        for m in range(1, 4):
            a2_copy(k, m).start()
            b2_copy(k, m).start()
        for m in range(1, 4):
            a2_copy(k, m).wait_recv()
            b2_copy(k, m).wait_recv()
        s4[k, grp, :64, :] = add_slots(a2, k, 4)
        s4[k, grp, 64:, :] = add_slots(b2, k, 4)
        for m in range(1, 4):
            y4_copy(k, m).start()
        c4_copy(k, 0).start()
        for m in range(1, 4):
            d1_copy(k, m).wait_recv()
        d2[k, xi] = add_slots(d1, k, 4)
        for m in range(1, 4):
            d2_copy(k, m).start()
        face_copy(k, 3).start()
        face_copy(k, 0).start()

        @pl.when(k == 0)
        def _():
            build_corners()

        @pl.when(k > 0)
        def _():
            follow(k - 1, beta_prev, alpha_prev)

        for m in range(1, 4):
            d2_copy(k, m).wait_recv()
        d3[k, grp] = add_slots(d2, k, 4)
        for m in range(1, 8):
            d3_copy(k, m).start()
        for m in range(1, 4):
            y4_copy(k, m).wait_recv()
            c4_copy(k, m).start()

        @pl.when(k == 0)
        def _():
            for copy in stage_x:
                copy.wait_recv()
            sibling.start()

        for f in ARRIVAL:
            face_copy(k, f).wait_recv()
            for s in range(2):
                for i in range(NF // 128):
                    rows = slice(f * NF + i * 128, f * NF + i * 128 + 128)
                    here = slice(i * 128, i * 128 + 128)
                    received = jnp.where(
                        flags[s][f],
                        frecv[k + 1, f, 1, here, :].astype(F32),
                        frecv[k + 1, f, 0, here, :].astype(F32),
                    )
                    frv[s, rows, :] = frv[s, rows, :] - received

        @pl.when(k == 0)
        def _():
            sibling.wait_recv()

        for m in range(4):
            c4_copy(k, m).wait_recv()

        for j in range(8):
            rows = slice(j * BLK, (j + 1) * BLK)
            high, low = halves(s4[k, j])
            rb2[rows, :LOADS] = high
            rb2[rows, LOADS:] = low
        quad = jnp.zeros((8, LOADS), F32)
        for j in range(8):
            rows = slice(j * BLK, (j + 1) * BLK)
            rhs = s4[k, j]
            y = dot(cg[0, rows, :HALF], rb2[:HALF, :]) + dot(cg[1, rows, :HALF], rb2[HALF:, :])
            y = y[:, :LOADS] + y[:, LOADS:] + cg[0, rows, HALF:].astype(F32) * rhs
            quad = quad + jnp.sum((y * rhs).reshape(16, 8, LOADS), axis=0)
            high, low = halves(y)
            yb[rows, :LOADS] = high
            yb[rows, LOADS:] = low
        quad = jnp.sum(quad, axis=0, keepdims=True)
        for m in range(1, 8):
            d3_copy(k, m).wait_recv()
        tile = add_slots(d3, k, 8)
        gamma = pick_row(tile, 0)
        delta = pick_row(tile, 1)
        picked = dot(oh[...], yb[...])
        cv[...] = picked[:, :LOADS] + picked[:, LOADS:]

        beta = jnp.where(k > 0, gamma / gamma_prev, 0.0)
        alpha = gamma / (2.0 * (delta + quad) - jnp.where(k > 0, beta * gamma / alpha_prev, 0.0))

        for f in range(FACES):
            for s in range(2):
                theirs = jnp.where(
                    flags[s][f],
                    cv[32 + 32 * f + 16 : 64 + 32 * f, :],
                    cv[32 + 32 * f : 48 + 32 * f, :],
                )
                mine_high, mine_low = halves(cv[16 * s : 16 * s + 16, :])
                high, low = halves(theirs)
                cc = jnp.concatenate([mine_high, high, mine_low, low, zeros64b], axis=0)
                for i in range(NF // 128):
                    rows = slice(f * NF + i * 128, f * NF + i * 128 + 128)
                    coarse = dot(bct[s, f, i * 128 : i * 128 + 128, :], cc)
                    u = frv[s, rows, :] + coarse + beta * uv[s, rows, :]
                    uv[s, rows, :] = u
                    r = rv[k, s, rows, :] - alpha * u
                    rv[k + 1, s, rows, :] = r
                    rb[s, rows, :] = r.astype(BF16)

        return gamma, alpha, beta

    ones = jnp.ones((1, LOADS), F32)
    _, alpha, beta = lax.fori_loop(0, ITERS, iteration, (ones, ones, ones))

    out_res = pltpu.make_async_copy(rv.at[ITERS], res_hbm, load_sem.at[10])
    out_res.start()
    follow(ITERS - 1, beta, alpha)
    out_mult = pltpu.make_async_copy(xv, mult_hbm, load_sem.at[9])
    out_mult.start()
    for k in range(ITERS):
        sent(k)
    for f in range(FACES):
        gap_copy(f, 0).wait_send()
        gap_copy(f, 1).wait_send()
    for copy in id_copies + b_copies:
        copy.wait_send()
    core_copy.wait_send()
    sibling.wait_send()
    for copy in stage_y + stage_z + stage_x:
        copy.wait_send()
    out_mult.wait()
    out_res.wait()


def shards(gap_loads, flexibility, corner_coupling, corner_ids, coarse_inverse, adjacency):
    ids = jnp.broadcast_to(corner_ids[:, :, None], corner_ids.shape + (LOADS,))
    field = jax.ShapeDtypeStruct((2, NI, LOADS), F32)
    vmem = pl.BlockSpec(memory_space=pltpu.VMEM)
    hbm = pl.BlockSpec(memory_space=pl.ANY)
    dma = pltpu.SemaphoreType.DMA
    return pl.pallas_call(
        kernel,
        out_shape=(field, field),
        in_specs=[pl.BlockSpec(memory_space=pltpu.SMEM), vmem, vmem, vmem, hbm, hbm],
        out_specs=(hbm, hbm),
        scratch_shapes=[
            pltpu.VMEM((2, NI, NI), BF16),
            pltpu.VMEM((2, NI, LOADS), BF16),
            pltpu.VMEM((ITERS + 1, 2, NI, LOADS), F32),
            pltpu.VMEM((2, NI, LOADS), F32),
            pltpu.VMEM((2, NI, LOADS), F32),
            pltpu.VMEM((2, NI, LOADS), F32),
            pltpu.VMEM((2, NI, LOADS), F32),
            pltpu.VMEM((2, NI, LOADS), BF16),
            pltpu.VMEM((ITERS + 1, FACES, 2, NF, LOADS), BF16),
            pltpu.VMEM((ITERS, FACES, 2, NF, LOADS), BF16),
            pltpu.VMEM((2, NCG, WIDE), BF16),
            pltpu.VMEM((8, NCG), F32),
            pltpu.VMEM((160, NCG), BF16),
            pltpu.VMEM((BLK, 2 * LOADS), BF16),
            pltpu.VMEM((2, FACES, NF, LOADS), BF16),
            pltpu.VMEM((8, 2, NC, LOADS), jnp.int32),
            pltpu.VMEM((2, NC, LOADS), jnp.int32),
            pltpu.VMEM((FACES, 2, NC, NF), BF16),
            pltpu.VMEM((ITERS, 8, 2 * NC, LOADS), BF16),
            pltpu.VMEM((ITERS, 4, 64, LOADS), F32),
            pltpu.VMEM((ITERS, 4, 64, LOADS), F32),
            pltpu.VMEM((ITERS, 4, 64, LOADS), F32),
            pltpu.VMEM((ITERS, 4, 64, LOADS), F32),
            pltpu.VMEM((ITERS, 4, 8, LOADS), F32),
            pltpu.VMEM((ITERS, 4, 8, LOADS), F32),
            pltpu.VMEM((ITERS, 8, 8, LOADS), F32),
            pltpu.VMEM((ITERS, 8, BLK, LOADS), F32),
            pltpu.VMEM((NCG, 2 * LOADS), BF16),
            pltpu.VMEM((NCG, 2 * LOADS), BF16),
            pltpu.VMEM((160, LOADS), F32),
            dma((12,)),
            dma((21,)),
            dma((21,)),
            dma((8,)),
            dma((8,)),
            dma((ITERS + 1, FACES)),
            dma((ITERS + 1, FACES)),
            dma((ITERS, 8)),
            dma((ITERS, 8)),
        ]
        + [dma((ITERS, 4))] * 12
        + [dma((ITERS, 8))] * 4
        + [dma((8,))] * 2,
        compiler_params=pltpu.CompilerParams(
            collective_id=0, has_side_effects=True, vmem_limit_bytes=60 * 1024 * 1024
        ),
    )(adjacency, ids, coarse_inverse, corner_coupling, gap_loads, flexibility)


def solution(mesh):
    return jax.shard_map(
        shards,
        mesh=mesh,
        in_specs=(
            P("sub", None, None),
            P("sub", None, None),
            P("sub", None, None),
            P("sub", None),
            P("sub", None),
            P("sub", None),
        ),
        out_specs=(P("sub", None, None), P("sub", None, None)),
        check_vma=False,
    )
```

```python
import jax
import jax.numpy as jnp
from jax import lax
from jax.experimental import pallas as pl
from jax.experimental.pallas import tpu as pltpu
from jax.sharding import PartitionSpec as P

ITERS = 3
FACES = 4
NF = 512
NI = 2048
NC = 16
LOADS = 128
NCG = 1024
BLK = 128
HALF = NCG // 2
WIDE = HALF + LOADS
FACE_ORDER = (2, 1, 3, 0)
ARRIVAL = (0, 3, 1, 2)
MESH = pl.DeviceIdType.MESH
F32 = jnp.float32
BF16 = jnp.bfloat16


def flip(index, mask):
    result = index
    bit = 1
    while bit <= mask:
        if mask & bit:
            result = result + bit * (1 - 2 * lax.rem(lax.div(index, bit), 2))
        bit *= 2
    return result


def dot(a, b):
    return jnp.dot(a, b, preferred_element_type=F32)


def sum_rows(gamma, delta):
    row = lax.broadcasted_iota(jnp.int32, (8, LOADS), 0)
    return jnp.where(row == 0, gamma, jnp.where(row == 1, delta, 0.0))


def pick_row(tile, index):
    row = lax.broadcasted_iota(jnp.int32, (8, LOADS), 0)
    return jnp.sum(jnp.where(row == index, tile, 0.0), axis=0, keepdims=True)


def halves(value):
    high = value.astype(BF16)
    return high, (value - high.astype(F32)).astype(BF16)


def kernel(
    adj_ref, raw_ref, cinv_ref, bc_ref, gap_hbm, flex_hbm,
    mult_hbm, res_hbm,
    fv, gapv, rv, pv, uv, xv, frv, rb, frecv, fsend,
    cg, cex, oh, scat, bct, ids_ref, idg, idz, brecv,
    s1, a1, a2, b1, b2, d1, d2, d3, s4, rb2, yb, cv,
    load_sem, send0, recv0, sendg, recvg, sendf, recvf, send1, recv1,
    senda1, recva1, senda2, recva2, sendb1, recvb1, sendb2, recvb2,
    sendd1, recvd1, sendd2, recvd2, sendd3, recvd3, send4, recv4, sendi, recvi,
):
    me = lax.axis_index("sub")
    core = lax.rem(me, 2)
    zi = lax.rem(lax.div(me, 8), 4)
    xi = lax.div(me, 32)
    chip = lax.div(me, 2)
    grp = lax.rem(me, 8)

    def remote(src, dst, send, recv, mask):
        return pltpu.make_async_remote_copy(
            src_ref=src, dst_ref=dst, send_sem=send, recv_sem=recv,
            device_id=(flip(me, mask),), device_id_type=MESH,
        )

    diagonal = lax.broadcasted_iota(jnp.int32, (NC, NC), 0) == lax.broadcasted_iota(jnp.int32, (NC, NC), 1)
    for s in range(2):
        row = jnp.broadcast_to(raw_ref[s : s + 1, :].astype(F32), (NC, NC))
        column = jnp.sum(jnp.where(diagonal, row, 0.0), axis=1, keepdims=True)
        ids_ref[s] = jnp.broadcast_to(column, (NC, LOADS))

    barrier = pltpu.get_barrier_semaphore()
    masks = [1, 2, 3, 4, 5, 6, 7, 8, 16, 24, 32, 64, 96]
    for mask in masks:
        pl.semaphore_signal(barrier, inc=1, device_id=(flip(me, mask),), device_id_type=MESH)
    pl.semaphore_wait(barrier, len(masks))

    def gap_copy(f, s):
        at = 2 * f + s
        return remote(
            gap_hbm.at[s, pl.ds(f * NF, NF), :], frecv.at[0, f, s], sendg.at[at], recvg.at[at], 1 << f
        )

    core_copy = remote(cinv_ref, cex, send0.at[0], recv0.at[0], 1)
    core_copy.start()
    gap_copy(2, 0).start()
    gap_copy(1, 0).start()
    gap_load = pltpu.make_async_copy(gap_hbm, gapv, load_sem.at[8])
    gap_load.start()

    id_copies = [
        remote(ids_ref, idg.at[grp], sendi.at[m], recvi.at[m], m) for m in range(1, 8)
    ] + [remote(ids_ref, idz, sendi.at[0], recvi.at[0], 8)]
    b_copies = [
        remote(bc_ref.at[:, :, pl.ds(f * NF, NF)], brecv.at[f], send0.at[5 + f], recv0.at[5 + f], 1 << f)
        for f in range(FACES)
    ]

    flex_loads = []
    for s in range(2):
        for f in range(FACES):
            load = pltpu.make_async_copy(
                flex_hbm.at[s, pl.ds(f * NF, NF)], fv.at[s, pl.ds(f * NF, NF)], load_sem.at[s * FACES + f]
            )
            load.start()
            flex_loads.append(load)

    def c_rows(rows, count):
        return cg.at[core, pl.ds(pl.multiple_of(rows, 16), count)]

    def c_stage(base, rows, count, unit):
        part = c_rows(rows, count)
        return [remote(part, part, send0.at[base + k], recv0.at[base + k], unit * k) for k in range(1, 4)]

    core_copy.wait_recv()
    own = cinv_ref[...]
    other = cex[...]
    even = jnp.where(core == 0, own, other)
    odd = jnp.where(core == 0, other, own)
    both = jnp.concatenate([even, odd], axis=0)
    half = jnp.where(core == 0, both[:, :HALF], both[:, HALF:])
    across = lax.broadcasted_iota(jnp.int32, (16, NCG), 1)
    down = lax.broadcasted_iota(jnp.int32, (16, NCG), 0)
    rest = both - both.astype(BF16).astype(F32)
    rest = jnp.sum(jnp.where(across == down + chip * 16, rest, 0.0), axis=1, keepdims=True)
    packed = jnp.concatenate([half, jnp.broadcast_to(rest, (16, LOADS))], axis=1)
    c_rows(chip * 16, 16)[...] = packed.astype(BF16)
    stage_y = c_stage(8, chip * 16, 16, 2)
    for copy in stage_y:
        copy.start()
    for f, s in ((2, 1), (1, 1), (3, 0), (3, 1), (0, 0), (0, 1)):
        gap_copy(f, s).start()
    for copy in id_copies + b_copies:
        copy.start()
    idg[grp] = ids_ref[...]

    lane = lax.broadcasted_iota(jnp.int32, (NC, LOADS), 1).astype(F32)

    def one_hot(ids):
        return [jnp.where(ids == lane + b * LOADS, 1.0, 0.0).astype(F32) for b in range(NCG // LOADS)]

    zeros64 = jnp.zeros((64, LOADS), F32)
    flags = [[lax.rem(adj_ref[s, f], 2) == 1 for f in range(FACES)] for s in range(2)]

    def spread(base, ids):
        hots = [one_hot(ids[s]) for s in range(2)]
        for b in range(NCG // LOADS):
            tile = jnp.concatenate([hots[0][b], hots[1][b]], axis=0)
            oh[base : base + 32, b * LOADS : (b + 1) * LOADS] = tile.astype(BF16)

    def build_scatter():
        for copy in id_copies:
            copy.wait_recv()
        mine = lane + (grp * BLK).astype(F32)
        for q in range(2):
            tiles = [
                jnp.where(idg[e, s] == mine, 1.0, 0.0).astype(F32)
                for e in range(4 * q, 4 * q + 4)
                for s in range(2)
            ]
            scat[:, q * LOADS : (q + 1) * LOADS] = jnp.concatenate(tiles, axis=0).T.astype(BF16)

    def build_corners():
        spread(0, ids_ref)
        for f in range(3):
            spread(32 + 32 * f, idg.at[flip(grp, 1 << f)])
        spread(32 + 32 * 3, idz)
        for f in range(FACES):
            b_copies[f].wait_recv()
            for s in range(2):
                for q in range(NF // LOADS):
                    cols = slice(q * LOADS, (q + 1) * LOADS)
                    mine = bc_ref[s, :, f * NF + q * LOADS : f * NF + (q + 1) * LOADS].astype(F32)
                    theirs = jnp.where(
                        flags[s][f], brecv[f, 1, :, cols].astype(F32), brecv[f, 0, :, cols].astype(F32)
                    )
                    tile = jnp.concatenate([mine, -theirs, mine, -theirs, zeros64], axis=0)
                    bct[s, f, cols, :] = tile.T.astype(BF16)

    def clear(i, carry):
        rows = pl.ds(pl.multiple_of(i * 64, 64), 64)
        for s in range(2):
            for ref in (pv, uv, xv):
                ref[s, rows, :] = jnp.zeros((64, LOADS), F32)
        return carry

    lax.fori_loop(0, NI // 64, clear, 0)

    for copy in stage_y:
        copy.wait_recv()
    stage_z = c_stage(12, lax.div(chip, 4) * 64, 64, 8)
    for copy in stage_z:
        copy.start()

    for copy in stage_z:
        copy.wait_recv()
    stage_x = c_stage(16, xi * 256, 256, 32)
    for copy in stage_x:
        copy.start()
    whole_c = cg.at[core]
    sibling = remote(whole_c, whole_c, send0.at[20], recv0.at[20], 1)

    gap_load.wait()
    for f in ARRIVAL:
        gap_copy(f, 0).wait_recv()
        gap_copy(f, 1).wait_recv()
        for s in range(2):
            for i in range(NF // 128):
                rows = slice(f * NF + i * 128, f * NF + i * 128 + 128)
                here = slice(i * 128, i * 128 + 128)
                mine = gapv[s, rows, :].astype(F32)
                theirs = jnp.where(
                    flags[s][f], frecv[0, f, 1, here, :].astype(F32), frecv[0, f, 0, here, :].astype(F32)
                )
                value = mine - theirs
                rv[0, s, rows, :] = value
                rb[s, rows, :] = value.astype(BF16)
    for load in flex_loads:
        load.wait()

    def face_copy(k, f):
        return remote(fsend.at[k, f], frecv.at[k + 1, f], sendf.at[k + 1, f], recvf.at[k + 1, f], 1 << f)

    def s1_copy(k, m):
        return remote(s1.at[k, grp], s1.at[k, grp], send1.at[k, m], recv1.at[k, m], m)

    def d3_copy(k, m):
        return remote(d3.at[k, grp], d3.at[k, grp], sendd3.at[k, m], recvd3.at[k, m], m)

    def a1_copy(k, m):
        return remote(a1.at[k, zi], a1.at[k, zi], senda1.at[k, m], recva1.at[k, m], 8 * m)

    def a2_copy(k, m):
        return remote(a2.at[k, xi], a2.at[k, xi], senda2.at[k, m], recva2.at[k, m], 32 * m)

    def b1_copy(k, m):
        return remote(b1.at[k, xi], b1.at[k, xi], sendb1.at[k, m], recvb1.at[k, m], 32 * m)

    def b2_copy(k, m):
        return remote(b2.at[k, zi], b2.at[k, zi], sendb2.at[k, m], recvb2.at[k, m], 8 * m)

    def d1_copy(k, m):
        return remote(d1.at[k, zi], d1.at[k, zi], sendd1.at[k, m], recvd1.at[k, m], 8 * m)

    def d2_copy(k, m):
        return remote(d2.at[k, xi], d2.at[k, xi], sendd2.at[k, m], recvd2.at[k, m], 32 * m)

    def y4_copy(k, m):
        return remote(s4.at[k, grp], s4.at[k, grp], send4.at[k, m], recv4.at[k, m], 2 * m)

    def c4_copy(k, m):
        block = s4.at[k, flip(grp, 2 * m)]
        return remote(block, block, send4.at[k, 4 + m], recv4.at[k, 4 + m], 1)

    zeros64b = jnp.zeros((64, LOADS), BF16)

    def sent(k):
        for f in range(FACES):
            face_copy(k, f).wait_send()
            c4_copy(k, f).wait_send()
        for m in range(1, 8):
            s1_copy(k, m).wait_send()
            d3_copy(k, m).wait_send()
        for m in range(1, 4):
            for copy in (a1_copy, a2_copy, b1_copy, b2_copy, d1_copy, d2_copy, y4_copy):
                copy(k, m).wait_send()

    def add_slots(ref, k, count):
        total = ref[k, 0].astype(F32)
        for i in range(1, count):
            total = total + ref[k, i].astype(F32)
        return total

    def follow(k, beta, alpha):
        for s in range(2):
            for i in range(NI // 128):
                rows = slice(i * 128, i * 128 + 128)
                p = rv[k, s, rows, :] + beta * pv[s, rows, :]
                pv[s, rows, :] = p
                xv[s, rows, :] = xv[s, rows, :] + alpha * p

    def iteration(k, carry):
        gamma_prev, alpha_prev, beta_prev = carry

        s1[k, grp] = jnp.concatenate([dot(bc_ref[s], rb[s]) for s in range(2)], axis=0).astype(BF16)
        for m in range(1, 8):
            s1_copy(k, m).start()

        gamma = jnp.zeros((8, LOADS), F32)
        delta = jnp.zeros((8, LOADS), F32)
        for place, f in enumerate(FACE_ORDER):
            for s in range(2):
                frv[s, f * NF : (f + 1) * NF, :] = dot(fv[s, f * NF : (f + 1) * NF, :], rb[s])
                for i in range(NF // 128):
                    rows = slice(f * NF + i * 128, f * NF + i * 128 + 128)
                    fr = frv[s, rows, :]
                    r = rv[k, s, rows, :]
                    fsend[k, f, s, i * 128 : i * 128 + 128, :] = fr.astype(BF16)
                    gamma = gamma + jnp.sum((r * r).reshape(16, 8, LOADS), axis=0)
                    delta = delta + jnp.sum((r * fr).reshape(16, 8, LOADS), axis=0)
            if f not in (0, 3):
                face_copy(k, f).start()
            if place == 1:

                @pl.when(k == 0)
                def _():
                    build_scatter()

                for m in range(1, 8):
                    s1_copy(k, m).wait_recv()
                total = dot(scat[...], s1[k].reshape(2 * BLK, LOADS))
                a1[k, zi] = total[:64]
                b1[k, xi] = total[64:]
                for m in range(1, 4):
                    a1_copy(k, m).start()
                    b1_copy(k, m).start()
        d1[k, zi] = sum_rows(
            jnp.sum(gamma, axis=0, keepdims=True), jnp.sum(delta, axis=0, keepdims=True)
        )
        for m in range(1, 4):
            d1_copy(k, m).start()

        for m in range(1, 4):
            a1_copy(k, m).wait_recv()
            b1_copy(k, m).wait_recv()
        a2[k, xi] = add_slots(a1, k, 4)
        b2[k, zi] = add_slots(b1, k, 4)
        for m in range(1, 4):
            a2_copy(k, m).start()
            b2_copy(k, m).start()
        for m in range(1, 4):
            a2_copy(k, m).wait_recv()
            b2_copy(k, m).wait_recv()
        s4[k, grp, :64, :] = add_slots(a2, k, 4)
        s4[k, grp, 64:, :] = add_slots(b2, k, 4)
        for m in range(1, 4):
            y4_copy(k, m).start()
        c4_copy(k, 0).start()
        for m in range(1, 4):
            d1_copy(k, m).wait_recv()
        d2[k, xi] = add_slots(d1, k, 4)
        for m in range(1, 4):
            d2_copy(k, m).start()
        face_copy(k, 3).start()
        face_copy(k, 0).start()

        @pl.when(k == 0)
        def _():
            build_corners()

        @pl.when(k > 0)
        def _():
            follow(k - 1, beta_prev, alpha_prev)

        for m in range(1, 4):
            d2_copy(k, m).wait_recv()
        d3[k, grp] = add_slots(d2, k, 4)
        for m in range(1, 8):
            d3_copy(k, m).start()
        for m in range(1, 4):
            y4_copy(k, m).wait_recv()
            c4_copy(k, m).start()

        @pl.when(k == 0)
        def _():
            for copy in stage_x:
                copy.wait_recv()
            sibling.start()

        for f in ARRIVAL:
            face_copy(k, f).wait_recv()
            for s in range(2):
                for i in range(NF // 128):
                    rows = slice(f * NF + i * 128, f * NF + i * 128 + 128)
                    here = slice(i * 128, i * 128 + 128)
                    received = jnp.where(
                        flags[s][f],
                        frecv[k + 1, f, 1, here, :].astype(F32),
                        frecv[k + 1, f, 0, here, :].astype(F32),
                    )
                    frv[s, rows, :] = frv[s, rows, :] - received

        @pl.when(k == 0)
        def _():
            sibling.wait_recv()

        for m in range(4):
            c4_copy(k, m).wait_recv()

        for j in range(8):
            rows = slice(j * BLK, (j + 1) * BLK)
            high, low = halves(s4[k, j])
            rb2[rows, :LOADS] = high
            rb2[rows, LOADS:] = low
        quad = jnp.zeros((8, LOADS), F32)
        for j in range(8):
            rows = slice(j * BLK, (j + 1) * BLK)
            rhs = s4[k, j]
            y = dot(cg[0, rows, :HALF], rb2[:HALF, :]) + dot(cg[1, rows, :HALF], rb2[HALF:, :])
            y = y[:, :LOADS] + y[:, LOADS:] + cg[0, rows, HALF:].astype(F32) * rhs
            quad = quad + jnp.sum((y * rhs).reshape(16, 8, LOADS), axis=0)
            high, low = halves(y)
            yb[rows, :LOADS] = high
            yb[rows, LOADS:] = low
        quad = jnp.sum(quad, axis=0, keepdims=True)
        for m in range(1, 8):
            d3_copy(k, m).wait_recv()
        tile = add_slots(d3, k, 8)
        gamma = pick_row(tile, 0)
        delta = pick_row(tile, 1)
        picked = dot(oh[...], yb[...])
        cv[...] = picked[:, :LOADS] + picked[:, LOADS:]

        beta = jnp.where(k > 0, gamma / gamma_prev, 0.0)
        alpha = gamma / (2.0 * (delta + quad) - jnp.where(k > 0, beta * gamma / alpha_prev, 0.0))

        for f in range(FACES):
            for s in range(2):
                theirs = jnp.where(
                    flags[s][f],
                    cv[32 + 32 * f + 16 : 64 + 32 * f, :],
                    cv[32 + 32 * f : 48 + 32 * f, :],
                )
                mine_high, mine_low = halves(cv[16 * s : 16 * s + 16, :])
                high, low = halves(theirs)
                cc = jnp.concatenate([mine_high, high, mine_low, low, zeros64b], axis=0)
                for i in range(NF // 128):
                    rows = slice(f * NF + i * 128, f * NF + i * 128 + 128)
                    coarse = dot(bct[s, f, i * 128 : i * 128 + 128, :], cc)
                    u = frv[s, rows, :] + coarse + beta * uv[s, rows, :]
                    uv[s, rows, :] = u
                    r = rv[k, s, rows, :] - alpha * u
                    rv[k + 1, s, rows, :] = r
                    rb[s, rows, :] = r.astype(BF16)

        return gamma, alpha, beta

    ones = jnp.ones((1, LOADS), F32)
    _, alpha, beta = lax.fori_loop(0, ITERS, iteration, (ones, ones, ones))

    out_res = pltpu.make_async_copy(rv.at[ITERS], res_hbm, load_sem.at[10])
    out_res.start()
    follow(ITERS - 1, beta, alpha)
    out_mult = pltpu.make_async_copy(xv, mult_hbm, load_sem.at[9])
    out_mult.start()
    for k in range(ITERS):
        sent(k)
    for f in range(FACES):
        gap_copy(f, 0).wait_send()
        gap_copy(f, 1).wait_send()
    for copy in id_copies + b_copies:
        copy.wait_send()
    core_copy.wait_send()
    sibling.wait_send()
    for copy in stage_y + stage_z + stage_x:
        copy.wait_send()
    out_mult.wait()
    out_res.wait()


def shards(gap_loads, flexibility, corner_coupling, corner_ids, coarse_inverse, adjacency):
    field = jax.ShapeDtypeStruct((2, NI, LOADS), F32)
    vmem = pl.BlockSpec(memory_space=pltpu.VMEM)
    hbm = pl.BlockSpec(memory_space=pl.ANY)
    dma = pltpu.SemaphoreType.DMA
    return pl.pallas_call(
        kernel,
        out_shape=(field, field),
        in_specs=[pl.BlockSpec(memory_space=pltpu.SMEM), vmem, vmem, vmem, hbm, hbm],
        out_specs=(hbm, hbm),
        scratch_shapes=[
            pltpu.VMEM((2, NI, NI), BF16),
            pltpu.VMEM((2, NI, LOADS), BF16),
            pltpu.VMEM((ITERS + 1, 2, NI, LOADS), F32),
            pltpu.VMEM((2, NI, LOADS), F32),
            pltpu.VMEM((2, NI, LOADS), F32),
            pltpu.VMEM((2, NI, LOADS), F32),
            pltpu.VMEM((2, NI, LOADS), F32),
            pltpu.VMEM((2, NI, LOADS), BF16),
            pltpu.VMEM((ITERS + 1, FACES, 2, NF, LOADS), BF16),
            pltpu.VMEM((ITERS, FACES, 2, NF, LOADS), BF16),
            pltpu.VMEM((2, NCG, WIDE), BF16),
            pltpu.VMEM((8, NCG), F32),
            pltpu.VMEM((160, NCG), BF16),
            pltpu.VMEM((BLK, 2 * LOADS), BF16),
            pltpu.VMEM((2, FACES, NF, LOADS), BF16),
            pltpu.VMEM((2, NC, LOADS), F32),
            pltpu.VMEM((8, 2, NC, LOADS), F32),
            pltpu.VMEM((2, NC, LOADS), F32),
            pltpu.VMEM((FACES, 2, NC, NF), BF16),
            pltpu.VMEM((ITERS, 8, 2 * NC, LOADS), BF16),
            pltpu.VMEM((ITERS, 4, 64, LOADS), F32),
            pltpu.VMEM((ITERS, 4, 64, LOADS), F32),
            pltpu.VMEM((ITERS, 4, 64, LOADS), F32),
            pltpu.VMEM((ITERS, 4, 64, LOADS), F32),
            pltpu.VMEM((ITERS, 4, 8, LOADS), F32),
            pltpu.VMEM((ITERS, 4, 8, LOADS), F32),
            pltpu.VMEM((ITERS, 8, 8, LOADS), F32),
            pltpu.VMEM((ITERS, 8, BLK, LOADS), F32),
            pltpu.VMEM((NCG, 2 * LOADS), BF16),
            pltpu.VMEM((NCG, 2 * LOADS), BF16),
            pltpu.VMEM((160, LOADS), F32),
            dma((12,)),
            dma((21,)),
            dma((21,)),
            dma((8,)),
            dma((8,)),
            dma((ITERS + 1, FACES)),
            dma((ITERS + 1, FACES)),
            dma((ITERS, 8)),
            dma((ITERS, 8)),
        ]
        + [dma((ITERS, 4))] * 12
        + [dma((ITERS, 8))] * 4
        + [dma((8,))] * 2,
        compiler_params=pltpu.CompilerParams(
            collective_id=0, has_side_effects=True, vmem_limit_bytes=60 * 1024 * 1024
        ),
    )(adjacency, corner_ids, coarse_inverse, corner_coupling, gap_loads, flexibility)


def solution(mesh):
    return jax.shard_map(
        shards,
        mesh=mesh,
        in_specs=(
            P("sub", None, None),
            P("sub", None, None),
            P("sub", None, None),
            P("sub", None),
            P("sub", None),
            P("sub", None),
        ),
        out_specs=(P("sub", None, None), P("sub", None, None)),
        check_vma=False,
    )
```
